256 devices in a mesh: dp: 16 (over z, core), expert: 16 (over x, y).
Axes of the slice: x: 4, y: 4, z: 8, core: 2. Of those that a mesh axis runs over, the one named last changes fastest.
Arguments:
- activations: bfloat16 [16384, 8, 768], P(('dp', 'expert')), may hold values from -6 to 6
- out_grad: bfloat16 [16384, 2048], P(('dp', 'expert')), may hold values from -0.796875 to 0.796875
- gate_weights: float32 [16384, 8], P(('dp', 'expert')), may hold values from 0.02 to 0.3
- routes: int32 [16384, 8], P(('dp', 'expert')), may hold values from 0 to 63, all different within a row; in each aligned block of 64 rows (0 to 63, 64 to 127, ...) at most 16 rows name the same one
- momentum: float32 [131072, 768], P(('expert', 'dp')), may hold values from -4 to 4
Outputs:
- update: bfloat16 [131072, 768], P(('expert', 'dp'))
- new_momentum: float32 [131072, 768], P(('expert', 'dp'))
The draws below stay inside these ranges and needn't reach their ends.
Inputs may be any that keep to these rules, and one draw needn't show every extreme that they name: `routes`: each row names 8 different experts. Among the 64 rows of one device no expert is named by more than 16 rows, and in every draw some expert is named by exactly 16 rows of some device.
All inputs are finite; a program needn't handle non-finite values.
Results may differ from the reference program's by a relative error of at most 0.029.
Values may be sent and summed in bfloat16 or wider, within the bound.
A program may use at most 128 MiB of HBM per device.

```python
import math
import jax
import jax.numpy as jnp
import numpy as np
from jax import lax

D = 2048
FF = 768
TOPK = 8
NS_ITERS = 2
TOK_DEV = 64
EXPERTS = 64
CAP = 16
TOKENS = 16384
N_DP = 16
N_EXPERT = 16


def block_levels(own_key, shape, shards, smallest, top_value):
    def one(axis_at, blocks):
        steps = jax.random.uniform(jax.random.fold_in(jax.random.fold_in(own_key, 6), axis_at), (blocks,), jnp.float32, smallest / len(shards), top_value / len(shards))
        return jnp.repeat(jnp.exp(steps), shape[axis_at] // blocks).reshape((-1,) + (1,) * (len(shape) - axis_at - 1))

    level = one(*shards[0])
    for cut in shards[1:]:
        level = level * one(*cut)
    return level


def routed_block(key, own, number, rows, amount, top, most, slope):
    ranking = jax.random.permutation(key, amount)
    crowded, common = shares(amount, rows * top, most, slope, True), shares(amount, rows * top, most, slope, False)
    places = jnp.arange(amount)

    def named(sizes, turn):
        used = int((sizes > 0).sum())
        fixed = max(1, used // 4)
        passed = fixed + (places - fixed + turn * (used - fixed)) % max(1, amount - fixed)
        return jnp.zeros((amount,), jnp.int32).at[ranking[jnp.where(places < fixed, places, passed)]].set(jnp.asarray(sizes, jnp.int32))

    sizes = jnp.where(number % 4 == 0, named(crowded, number // 4), named(common, number - number // 4 - 1))
    mixed = jax.random.permutation(jax.random.fold_in(own, 3), amount)
    giver, taker = mixed[0:amount // 2 * 2:2], mixed[1:amount // 2 * 2:2]
    margin = jnp.minimum(sizes[giver] - 1, most - sizes[taker]) // 2
    margin = jnp.where((giver == ranking[0]) | (taker == ranking[0]) | (sizes[taker] == 0), 0, jnp.maximum(margin, 0))
    passed = jax.random.randint(jax.random.fold_in(own, 4), (amount // 2,), 0, 1 << 20) % (margin + 1)
    sizes = sizes.at[giver].add(-passed).at[taker].add(passed)
    labels = jnp.searchsorted(jnp.cumsum(sizes), jnp.arange(rows * top), side="right").astype(jnp.int32)
    table = labels.reshape(top, rows).T
    table = table[jax.random.permutation(jax.random.fold_in(own, 1), rows)]
    turn = jax.random.randint(jax.random.fold_in(own, 2), (rows, 1), 0, top)
    return jnp.take_along_axis(table, (jnp.arange(top)[None, :] + turn) % top, axis=1)


def shares(amount, total, bound, slope, full):
    weights = [(1 << 20) // math.isqrt(standing ** slope) + 1 for standing in range(1, amount + 1)]
    largest = bound if full else min(bound, max(-(-total // amount), total * weights[0] // sum(weights)))
    least = 1 if total - largest >= amount - 1 else 0
    given, spare = [largest] + [least] * (amount - 1), total - largest - least * (amount - 1)
    while spare > 0:
        free = [i for i in range(1, amount) if given[i] < largest] or [i for i in range(1, amount) if given[i] < bound]
        mass, budget = sum([weights[i] for i in free]), spare
        for i in free:
            extra = min(bound - given[i], max(1, budget * weights[i] // mass), spare)
            given[i] = given[i] + extra
            spare = spare - extra
    return np.array(given)


def normal_values(key, dims, spread, reach, split=(), kind=jnp.bfloat16):
    values = spread * jax.random.normal(key, dims, jnp.float32)
    if split:
        values = values * block_levels(key, dims, split, -0.22, 0.18)
    return jnp.clip(values, -reach, reach).astype(kind)


def setup_inputs(seed: int = 0) -> dict:
    streams_of = jax.random.split(jax.random.key(seed), 6)
    activations = normal_values(streams_of[0], (TOKENS, TOPK, FF), 1.0, 6.0, ((0, 256),))
    out_grad = normal_values(streams_of[1], (TOKENS, D), 0.1, 0.796875, ((0, 256),))
    gate_weights = jnp.clip(jnp.exp(math.log(0.3) - 2.7080503 * jax.random.uniform(streams_of[2], (TOKENS, TOPK), jnp.float32) ** block_levels(streams_of[2], (TOKENS, TOPK), ((0, 256),), -0.2, 0.2)), 0.02, 0.3)
    routes_keys = jax.random.split(jax.random.fold_in(streams_of[3], 1), TOKENS // TOK_DEV)
    routes_turns = jax.random.permutation(jax.random.fold_in(streams_of[3], 3), TOKENS // TOK_DEV)
    routes = jax.vmap(lambda own, number: routed_block(jax.random.fold_in(streams_of[3], 2), own, number, TOK_DEV, EXPERTS, TOPK, CAP, 2))(routes_keys, routes_turns).reshape((TOKENS, TOPK))
    momentum = normal_values(streams_of[4], (EXPERTS * D, FF), 0.5, 4.0, ((0, 256),), jnp.float32)
    return {"activations": activations, "out_grad": out_grad, "gate_weights": gate_weights, "routes": routes, "momentum": momentum}


MOMENT = 0.95
COEFF_A = 3.4445
COEFF_B = -4.775
COEFF_C = 2.0315
EPSILON = 1e-07

def slot_table(routing, expert_total, capacity):
    tokens_here = routing.shape[0]
    slots_token = routing.shape[1]
    numbers = jnp.arange(expert_total, dtype=jnp.int32)
    matched = (routing[:, :, None] == numbers[None, None, :]).astype(jnp.int32)
    named_by = lax.optimization_barrier(jnp.sum(matched, axis=1))
    position = lax.optimization_barrier(jnp.sum(matched * jnp.arange(slots_token, dtype=jnp.int32)[None, :, None], axis=1))
    earlier = jnp.cumsum(named_by, axis=0) - named_by
    places = jnp.arange(capacity, dtype=jnp.int32)
    picked = ((named_by[:, :, None] == 1) & (earlier[:, :, None] == places[None, None, :])).astype(jnp.int32)
    pair_index = jnp.arange(tokens_here, dtype=jnp.int32)[:, None] * slots_token + position
    source = lax.optimization_barrier(jnp.sum(picked * pair_index[:, :, None], axis=0)).astype(jnp.int32)
    filled = lax.optimization_barrier(jnp.sum(picked, axis=0)) > 0
    return (source, filled)

def pack_slots(hidden_block, grad_block, gate_block, source, filled, slots_token):
    hidden_rows = hidden_block.reshape(-1, hidden_block.shape[-1])
    picked_rows = jnp.where(filled[..., None], jnp.take(hidden_rows, source, axis=0), jnp.zeros((), hidden_rows.dtype))
    scales = jnp.where(filled, jnp.take(gate_block.reshape(-1), source), jnp.zeros((), jnp.float32))
    grad_rows = jnp.take(grad_block, source // slots_token, axis=0).astype(jnp.float32)
    weighted = (scales[..., None] * grad_rows).astype(jnp.bfloat16)
    return (picked_rows, weighted)

def device_slots(hidden_block, grad_block, gate_block, route_block):
    source, filled = slot_table(route_block, EXPERTS, CAP)
    return pack_slots(hidden_block, grad_block, gate_block, source, filled, TOPK)

def newton_update(scaled, gram):
    square = jnp.dot(gram, gram, preferred_element_type=jnp.float32)
    poly = (COEFF_B * gram.astype(jnp.float32) + COEFF_C * square).astype(jnp.bfloat16)
    product = jnp.dot(scaled, poly, preferred_element_type=jnp.float32)
    return (COEFF_A * scaled.astype(jnp.float32) + product).astype(jnp.bfloat16)

def orthogonal(ahead):
    norm_value = jnp.sqrt(jnp.sum(ahead * ahead))
    scaled = (ahead / (norm_value + EPSILON)).astype(jnp.bfloat16)
    for turn_index in range(NS_ITERS):
        gram = lax.dot_general(scaled, scaled, (((0,), (0,)), ((), ())), preferred_element_type=jnp.float32).astype(jnp.bfloat16)
        scaled = newton_update(scaled, gram)
    return (math.sqrt(D) * scaled.astype(jnp.float32)).astype(jnp.bfloat16)

def reference(activations, out_grad, gate_weights, routes, momentum):
    hidden = activations.reshape(N_DP, N_EXPERT, TOK_DEV, TOPK, FF)
    grads = out_grad.reshape(N_DP, N_EXPERT, TOK_DEV, D)
    gates = gate_weights.reshape(N_DP, N_EXPERT, TOK_DEV, TOPK)
    routing = routes.reshape(N_DP, N_EXPERT, TOK_DEV, TOPK)

    def add_rank(running, inputs):
        hidden_rank, grad_rank, gate_rank, route_rank = inputs
        slot_rows, slot_weighted = jax.vmap(device_slots)(hidden_rank, grad_rank, gate_rank, route_rank)
        partial_value = jnp.einsum('qecd,qecf->edf', slot_weighted.astype(jnp.float32), slot_rows.astype(jnp.float32), precision=lax.Precision.HIGHEST)
        rounded = lax.optimization_barrier(partial_value.astype(jnp.bfloat16))
        return (running + rounded.astype(jnp.float32), None)
    start_sum = jnp.zeros((EXPERTS, D, FF), jnp.float32)
    gradient, unused = lax.scan(add_rank, start_sum, (hidden, grads, gates, routing))
    previous = momentum.reshape(EXPERTS, D, FF)
    new_momentum = MOMENT * previous + gradient
    ahead = gradient + MOMENT * new_momentum
    update = lax.map(orthogonal, ahead)
    return (update.reshape(EXPERTS * D, FF), new_momentum.reshape(EXPERTS * D, FF))
```

```python
import math

import jax
import jax.numpy as jnp
from jax import lax
from jax.experimental import pallas as pl
from jax.experimental.pallas import tpu as pltpu
from jax.sharding import PartitionSpec as P

MOMENT = 0.95
COEFF_A = 3.4445
COEFF_B = -4.775
COEFF_C = 2.0315
EPSILON = 1e-07

F32, BF16, I32 = jnp.float32, jnp.bfloat16, jnp.int32
MESH = pl.DeviceIdType.MESH
D, FF, TOK, TOPK, CAP = 2048, 768, 64, 8, 16
PLANE, RING, SIDE = 16, 8, 4
PAIRS = TOK * TOPK
ROWS = 512
HALF = 256
BLK = 256
PARTS = (((0, 0), (0, 1), (1, 1)), ((0, 2), (1, 2), (2, 2)))


def iota(shape, dim):
    return lax.broadcasted_iota(I32, shape, dim)


def dot(a, b):
    return jnp.dot(a, b, preferred_element_type=F32)


def kernel(
    act,
    og,
    gate,
    routes,
    mom_hbm,
    update,
    new_mom,
    mom,
    ogx,
    og_buf,
    a_send,
    a_buf,
    idx_mine,
    idx_peer,
    idx_send,
    idx_buf,
    sel,
    wt,
    first,
    ring,
    xs,
    gram_part,
    gram_out,
    gram_core,
    gram_sum,
    gram_z,
    gram_tot,
    gram,
    poly,
    hmat,
    hmat16,
    x1,
    local_sem,
    ogx_send,
    ogx_recv,
    og_send,
    og_recv,
    a_send_sem,
    a_recv_sem,
    a_own_sem,
    ap_send,
    ap_recv,
    idx_sems,
    idx_all_send,
    idx_all_recv,
    z_send,
    z_recv,
    g_send,
    g_recv,
):
    dp = lax.axis_index("dp")
    q = lax.axis_index("expert")
    z, c = lax.div(dp, 2), lax.rem(dp, 2)
    g0, zo = lax.div(z, 2), lax.rem(z, 2)
    qx, qy = lax.div(q, SIDE), lax.rem(q, SIDE)
    peer = 2 * z + 1 - c
    zr = 2 * lax.rem(z + 1, RING) + c
    zl = 2 * lax.rem(z + RING - 1, RING) + c
    zpair = 2 * (2 * g0 + 1 - zo) + c

    def send(src, dst, s_sem, r_sem, to_dp, to_q):
        copy = pltpu.make_async_remote_copy(
            src_ref=src,
            dst_ref=dst,
            send_sem=s_sem,
            recv_sem=r_sem,
            device_id=(to_dp, to_q),
            device_id_type=MESH,
        )
        copy.start()
        return copy

    pending = []
    mom_copy = pltpu.make_async_copy(mom_hbm, mom, local_sem.at[0])
    mom_copy.start()

    barrier = pltpu.get_barrier_semaphore()

    def greet(i, carry):
        pl.semaphore_signal(
            barrier, inc=1, device_id=(dp, lax.rem(q + i, PLANE)), device_id_type=MESH
        )
        return carry

    lax.fori_loop(1, PLANE, greet, 0)
    for other in (peer, zr, zl):
        pl.semaphore_signal(barrier, inc=1, device_id=(other, q), device_id_type=MESH)
    pl.semaphore_wait(barrier, PLANE + 2)

    swaps, owns = [], []
    for o in range(2):
        zp = zo if o == 0 else 1 - zo
        mine = pl.multiple_of((2 * zp + c) * ROWS, ROWS)
        theirs = pl.multiple_of((2 * zp + 1 - c) * ROWS, ROWS)
        swaps.append(
            send(
                og.at[:, pl.ds(theirs, ROWS)],
                ogx.at[o, c],
                ogx_send.at[o],
                ogx_recv.at[o],
                peer,
                q,
            )
        )
        own = pltpu.make_async_copy(
            og.at[:, pl.ds(mine, ROWS)], ogx.at[o, c], local_sem.at[1 + o]
        )
        own.start()
        owns.append(own)

    spread = (lax.shift_right_logical(iota((TOK, PAIRS), 1), 3) == iota((TOK, PAIRS), 0)).astype(
        F32
    )
    own_k = (iota((TOPK, PAIRS), 1) & 7) == iota((TOPK, PAIRS), 0)

    def as_row(values):
        wide = lax.dot_general(
            values,
            spread,
            (((0,), (0,)), ((), ())),
            precision=lax.Precision.HIGHEST,
            preferred_element_type=F32,
        )
        return jnp.sum(jnp.where(own_k, wide, 0.0), axis=0, keepdims=True)

    route_row = as_row(routes[...].astype(F32))
    gate_row = as_row(gate[...])
    named = iota((TOK, PAIRS), 0).astype(F32) == route_row
    before = lax.shift_right_logical(iota((PAIRS, PAIRS), 0), 3) < lax.shift_right_logical(
        iota((PAIRS, PAIRS), 1), 3
    )
    counts = dot(named.astype(F32).astype(BF16), before.astype(F32).astype(BF16))
    place = jnp.sum(jnp.where(named, counts, 0.0), axis=0, keepdims=True)
    route_int = route_row.astype(I32)
    place_int = place.astype(I32)
    route_low, route_high = route_int & 3, lax.shift_right_logical(route_int, 2)
    slot = route_low * (PLANE * CAP) + route_high * CAP + place_int

    g_at = (
        lax.rem(g0 + 2, 4),
        lax.rem(g0 + 1 + 2 * zo, 4),
        lax.rem(g0 + 3 - 2 * zo, 4),
        g0,
    )

    def pack(pos):
        hit = (iota((PLANE * CAP, PAIRS), 0) + g_at[pos] * (PLANE * CAP)) == slot
        picked = dot(hit.astype(F32).astype(BF16), act[...])
        scale = jnp.sum(jnp.where(hit, gate_row, 0.0), axis=1, keepdims=True)
        a_send[pos] = (picked * scale).astype(BF16)

        def one(i, carry):
            to = lax.rem(q + i, PLANE)
            send(
                a_send.at[pos, pl.ds(pl.multiple_of(to * CAP, CAP), CAP)],
                a_buf.at[pos, qx, c, pl.ds(pl.multiple_of(qy * CAP, CAP), CAP)],
                a_send_sem.at[pos],
                a_recv_sem.at[pos],
                dp,
                to,
            )
            return carry

        lax.fori_loop(1, PLANE, one, 0)
        pltpu.make_async_copy(
            a_send.at[pos, pl.ds(pl.multiple_of(q * CAP, CAP), CAP)],
            a_buf.at[pos, qx, c, pl.ds(pl.multiple_of(qy * CAP, CAP), CAP)],
            a_own_sem.at[pos],
        ).start()

    def forward(pos):
        rest = a_send.at[pos, pl.ds(0, (PLANE - 1) * CAP)]
        pltpu.make_async_copy(rest, rest, a_recv_sem.at[pos]).wait()
        piece = a_send.at[pos, pl.ds(0, CAP)]
        pltpu.make_async_copy(piece, piece, a_own_sem.at[pos]).wait()
        copy = send(
            a_buf.at[pos, :, c], a_buf.at[pos, :, c], ap_send.at[pos], ap_recv.at[pos], peer, q
        )
        pending.append(copy)
        return copy

    u, v = (1 - c) * qx + c * qy, (1 - c) * qy + c * qx

    def at(du, dv):
        uu, vv = lax.rem(u + du + SIDE, SIDE), lax.rem(v + dv + SIDE, SIDE)
        return (1 - c) * (SIDE * uu + vv) + c * (SIDE * vv + uu)

    def og_send_one(o, source, to, key):
        pending.append(
            send(
                og_buf.at[o, source],
                og_buf.at[o, source],
                og_send.at[o, key],
                og_recv.at[o, key],
                dp,
                to,
            )
        )

    def og_wait(o, source, key):
        pltpu.make_async_remote_copy(
            src_ref=og_buf.at[o, source],
            dst_ref=og_buf.at[o, source],
            send_sem=og_send.at[o, key],
            recv_sem=og_recv.at[o, key],
            device_id=(dp, q),
            device_id_type=MESH,
        ).wait_recv()

    k_du = (0, -1, 1, 2)

    def og_begin(o):
        swaps[o].wait_recv()
        owns[o].wait()
        rows = ogx[o].reshape(2 * TOK, ROWS)
        og_buf[o, q] = rows.T
        og_send_one(o, q, at(1, 0), 0)
        og_send_one(o, q, at(-1, 0), 1)
        og_send_one(o, q, at(0, 1), 3)
        og_send_one(o, q, at(0, -1), 7)

    def og_second(o, k):
        source = at(k_du[k], 0)
        og_send_one(o, source, at(0, 1), 3 + k)
        og_send_one(o, source, at(0, -1), 7 + k)

    def og_relay(o, k):
        if k < 2:
            og_wait(o, at(k_du[k], -1), 3 + k)
            og_send_one(o, at(k_du[k], -1), at(0, 1), 11 + k)
        else:
            og_wait(o, at(k_du[k], 1), 7 + k)
            og_send_one(o, at(k_du[k], 1), at(0, -1), 11 + k)

    def og_middle(o):
        og_wait(o, at(-1, 0), 0)
        if o == 0:
            og_send_one(o, at(-1, 0), at(1, 0), 2)
        og_second(o, 1)
        og_wait(o, at(1, 0), 1)
        if o == 1:
            og_send_one(o, at(1, 0), at(-1, 0), 2)
        og_second(o, 2)
        og_relay(o, 0)

    def og_end(o):
        og_wait(o, at(2, 0), 2)
        og_second(o, 3)
        for k in (1, 2, 3):
            og_relay(o, k)
        for k in (2, 3):
            og_wait(o, at(k_du[k], -1), 3 + k)
        for k in (0, 1):
            og_wait(o, at(k_du[k], 1), 7 + k)
        for k in range(4):
            og_wait(o, at(k_du[k], 2), 11 + k)

    og_begin(0)
    pack(0)

    key_row = route_low * CAP + place_int
    token = lax.shift_right_logical(iota((TOK, PAIRS), 1), 3) + 1 + TOK * c
    key_hot = jnp.where(iota((TOK, PAIRS), 0) == key_row, token, 0).astype(F32).astype(BF16)
    high_hot = (iota((PLANE, PAIRS), 0) == route_high).astype(F32).astype(BF16)
    tokens = lax.dot_general(
        high_hot, key_hot, (((1,), (1,)), ((), ())), preferred_element_type=F32
    )
    lane = iota((TOK, PAIRS), 1)
    lane_key = lax.shift_right_logical(lane, 7) * CAP + (lane & 15)
    lane_mine = ((lax.shift_right_logical(lane, 6) & 1) == c) & (
        (lax.shift_right_logical(lane, 4) & 3) == qy
    )
    widen = (lane_mine & (lane_key == iota((TOK, PAIRS), 0))).astype(F32).astype(BF16)
    idx_mine[...] = dot(tokens.astype(BF16), widen)
    idx_swap = send(idx_mine, idx_peer, idx_sems.at[0], idx_sems.at[1], peer, q)

    og_middle(0)

    idx_swap.wait_recv()
    both = idx_mine[...] + idx_peer[...]
    for i in range(PLANE):
        idx_send[i] = both[i : i + 1]

    def idx_one(i, carry):
        to = lax.rem(q + i, PLANE)
        send(idx_send.at[to], idx_buf.at[q], idx_all_send.at[to], idx_all_recv.at[q], dp, to)
        return carry

    lax.fori_loop(1, PLANE, idx_one, 0)
    idx_buf[q] = idx_send[q]

    pack(1)
    og_begin(1)
    og_end(0)
    pack(2)
    pack(3)
    og_middle(1)

    def idx_wait(i, carry):
        source = lax.rem(q + i, PLANE)
        pltpu.make_async_copy(
            idx_buf.at[source], idx_buf.at[source], idx_all_recv.at[source]
        ).wait()
        return carry

    lax.fori_loop(1, PLANE, idx_wait, 0)

    for grp in range(4):
        for j in range(4):
            hit = (iota((2 * TOK, PAIRS), 0) + 1).astype(F32) == idx_buf[4 * grp + j]
            sel[grp, j * 128 : (j + 1) * 128] = hit.astype(F32).astype(BF16)

    def pick(o):
        def tile(t, carry):
            rows = pl.ds(pl.multiple_of(t * 128, 128), 128)
            for grp in range(4):
                left = jnp.concatenate([og_buf[o, 4 * grp + j, rows] for j in range(4)], axis=1)
                out = dot(left, sel[grp]).astype(BF16)
                for g in range(4):
                    wt[g, o, rows, grp * 128 : (grp + 1) * 128] = out[:, g * 128 : (g + 1) * 128]
            return carry

        lax.fori_loop(0, 4, tile, 0)

    def partial(g, o, pos, low, n):
        cols = slice(n * BLK, (n + 1) * BLK)
        return dot(wt[g, o, low : low + HALF], a_buf[pos, :, :, :, cols].reshape(PAIRS, BLK))

    def half_step(h):
        dist = (4, 3, 3, 2, 2, 1, 1)[h]
        o = (0, 1, 1, 0, 0, 1, 1)[h]
        place_right = (0, 1 - zo, 1 - zo, 1 + zo, 1 + zo, 3 - zo, 3 - zo)[h]
        place_left = (0, zo, zo, 2 - zo, 2 - zo, 2 + zo, 2 + zo)[h]
        for way in range(2):
            dest = lax.rem(z + (dist if way == 0 else RING - dist), RING)
            g = lax.div(dest, 2)
            pos = place_right if way == 0 else place_left
            low = HALF * ((h + way) % 2)
            target = first.at[way, h] if h < 2 else ring.at[way, h - 2]
            if h >= 2:
                z_copies[way][h - 2].wait_recv()
            for n in range(3):
                cols = slice(n * BLK, (n + 1) * BLK)
                value = partial(g, o, pos, low, n)
                if h >= 2:
                    value = value + ring[way, h - 2, :, cols].astype(F32)
                target[:, cols] = value.astype(BF16)
            copy = send(
                target,
                ring.at[way, h],
                z_send.at[way, h],
                z_recv.at[way, h],
                zr if way == 0 else zl,
                q,
            )
            pending.append(copy)
            z_copies[way].append(copy)

    z_copies = ([], [])
    pick(0)
    arrive = [forward(0)]
    arrive[0].wait_recv()
    half_step(0)

    og_end(1)
    pick(1)
    arrive.append(forward(1))
    arrive[1].wait_recv()
    half_step(1)
    arrive.append(forward(2))
    arrive.append(forward(3))
    half_step(2)
    arrive[2].wait_recv()
    half_step(3)
    half_step(4)
    arrive[3].wait_recv()
    half_step(5)
    half_step(6)

    mom_copy.wait()
    for way in range(2):
        z_copies[way][5].wait_recv()
    for way in range(2):
        z_copies[way][6].wait_recv()
    for top in range(2):
        rows = slice(top * HALF, (top + 1) * HALF)
        for n in range(3):
            cols = slice(n * BLK, (n + 1) * BLK)
            gradient = (
                partial(g0, 0, 3, top * HALF, n)
                + ring[0, 6 - top, :, cols].astype(F32)
                + ring[1, 5 + top, :, cols].astype(F32)
            )
            momentum = MOMENT * mom[rows, cols] + gradient
            new_mom[rows, cols] = momentum
            xs[rows, cols] = (gradient + MOMENT * momentum).astype(BF16)

    for half in range(2):
        for i, (a, b) in enumerate(PARTS[half]):
            gram_part[half, i] = lax.dot_general(
                xs[:, a * BLK : (a + 1) * BLK],
                xs[:, b * BLK : (b + 1) * BLK],
                (((0,), (0,)), ((), ())),
                preferred_element_type=F32,
            )
    gram_out[...] = gram_part[1 - c].astype(BF16)
    to_core = send(gram_out, gram_core, g_send.at[0], g_recv.at[0], peer, q)
    pending.append(to_core)
    to_core.wait_recv()
    gram_sum[...] = (gram_part[c] + gram_core[...].astype(F32)).astype(BF16)
    to_z = send(gram_sum, gram_z, g_send.at[1], g_recv.at[1], zpair, q)
    pending.append(to_z)
    to_z.wait_recv()
    gram_tot[c] = (gram_sum[...].astype(F32) + gram_z[...].astype(F32)).astype(BF16)
    back = send(gram_tot.at[c], gram_tot.at[c], g_send.at[2], g_recv.at[2], peer, q)
    pending.append(back)
    back.wait_recv()

    trace = jnp.zeros((1, 1), F32)
    eye = iota((BLK, BLK), 0) == iota((BLK, BLK), 1)
    for half in range(2):
        for i, (a, b) in enumerate(PARTS[half]):
            block = gram_tot[half, i]
            gram[a * BLK : (a + 1) * BLK, b * BLK : (b + 1) * BLK] = block
            wide = block.astype(F32)
            if a == b:
                trace = trace + jnp.sum(
                    jnp.sum(jnp.where(eye, wide, 0.0), axis=1, keepdims=True), axis=0, keepdims=True
                )
            else:
                gram[b * BLK : (b + 1) * BLK, a * BLK : (a + 1) * BLK] = wide.T.astype(BF16)
    scale = 1.0 / (jnp.sqrt(trace) + EPSILON)
    scale2 = scale * scale

    def rows_of(t):
        return slice(t * BLK, (t + 1) * BLK)

    for t in range(3):
        square = dot(gram[rows_of(t)], gram[...])
        poly[rows_of(t)] = (
            (COEFF_B * scale2) * gram[rows_of(t)].astype(F32)
            + (COEFF_C * scale2 * scale2) * square
        ).astype(BF16)
    for t in range(3):
        value = scale2 * (
            COEFF_A * gram[rows_of(t)].astype(F32) + dot(poly[rows_of(t)], gram[...])
        )
        hmat[rows_of(t)] = value
        hmat16[rows_of(t)] = value.astype(BF16)
    for t in range(2):
        value = COEFF_A * xs[rows_of(t)].astype(F32) + dot(xs[rows_of(t)], poly[...])
        x1[rows_of(t)] = (scale * value).astype(BF16)
    for t in range(3):
        value = COEFF_A * hmat[rows_of(t)] + dot(hmat16[rows_of(t)], poly[...])
        gram[rows_of(t)] = value.astype(BF16)
    for t in range(3):
        square = dot(gram[rows_of(t)], gram[...])
        hmat16[rows_of(t)] = (
            COEFF_B * gram[rows_of(t)].astype(F32) + COEFF_C * square
        ).astype(BF16)
    for t in range(2):
        value = COEFF_A * x1[rows_of(t)].astype(F32) + dot(x1[rows_of(t)], hmat16[...])
        update[rows_of(t)] = (math.sqrt(D) * value.astype(BF16).astype(F32)).astype(BF16)

    for copy in swaps + [idx_swap] + pending:
        copy.wait_send()
    for pos in range(4):
        rest = a_send.at[pos, pl.ds(0, (PLANE - 1) * CAP)]
        pltpu.make_async_copy(rest, rest, a_send_sem.at[pos]).wait()

    def idx_done(i, carry):
        to = lax.rem(q + i, PLANE)
        pltpu.make_async_copy(idx_send.at[to], idx_send.at[to], idx_all_send.at[to]).wait()
        return carry

    lax.fori_loop(1, PLANE, idx_done, 0)


def body(activations, out_grad, gate_weights, routes, momentum):
    vmem = pl.BlockSpec(memory_space=pltpu.VMEM)
    dma = pltpu.SemaphoreType.DMA
    scratch = [
        pltpu.VMEM((ROWS, FF), F32),
        pltpu.VMEM((2, 2, TOK, ROWS), BF16),
        pltpu.VMEM((2, PLANE, ROWS, 2 * TOK), BF16),
        pltpu.VMEM((4, PLANE * CAP, FF), BF16),
        pltpu.VMEM((4, 4, 2, 4 * CAP, FF), BF16),
        pltpu.VMEM((PLANE, PAIRS), F32),
        pltpu.VMEM((PLANE, PAIRS), F32),
        pltpu.VMEM((PLANE, 1, PAIRS), F32),
        pltpu.VMEM((PLANE, 1, PAIRS), F32),
        pltpu.VMEM((4, PAIRS, PAIRS), BF16),
        pltpu.VMEM((4, 2, ROWS, PAIRS), BF16),
        pltpu.VMEM((2, 2, HALF, FF), BF16),
        pltpu.VMEM((2, 7, HALF, FF), BF16),
        pltpu.VMEM((ROWS, FF), BF16),
        pltpu.VMEM((2, 3, BLK, BLK), F32),
        pltpu.VMEM((3, BLK, BLK), BF16),
        pltpu.VMEM((3, BLK, BLK), BF16),
        pltpu.VMEM((3, BLK, BLK), BF16),
        pltpu.VMEM((3, BLK, BLK), BF16),
        pltpu.VMEM((2, 3, BLK, BLK), BF16),
        pltpu.VMEM((FF, FF), BF16),
        pltpu.VMEM((FF, FF), BF16),
        pltpu.VMEM((FF, FF), F32),
        pltpu.VMEM((FF, FF), BF16),
        pltpu.VMEM((ROWS, FF), BF16),
        dma((3,)),
        dma((2,)),
        dma((2,)),
        dma((2, 15)),
        dma((2, 15)),
        dma((4,)),
        dma((4,)),
        dma((4,)),
        dma((4,)),
        dma((4,)),
        dma((2,)),
        dma((PLANE,)),
        dma((PLANE,)),
        dma((2, 7)),
        dma((2, 7)),
        dma((3,)),
        dma((3,)),
    ]
    return pl.pallas_call(
        kernel,
        out_shape=(
            jax.ShapeDtypeStruct((ROWS, FF), BF16),
            jax.ShapeDtypeStruct((ROWS, FF), F32),
        ),
        in_specs=[vmem] * 4 + [pl.BlockSpec(memory_space=pl.ANY)],
        out_specs=(vmem, vmem),
        scratch_shapes=scratch,
        compiler_params=pltpu.CompilerParams(
            collective_id=0, has_side_effects=True, vmem_limit_bytes=56 * 2**20
        ),
    )(activations.reshape(PAIRS, FF), out_grad, gate_weights, routes, momentum)


def solution(mesh):
    in_specs = (
        P(("dp", "expert"), None, None),
        P(("dp", "expert"), None),
        P(("dp", "expert"), None),
        P(("dp", "expert"), None),
        P(("expert", "dp"), None),
    )
    out_specs = (P(("expert", "dp"), None), P(("expert", "dp"), None))
    return jax.shard_map(body, mesh=mesh, in_specs=in_specs, out_specs=out_specs, check_vma=False)
```

```python
import math

import jax
import jax.numpy as jnp
from jax import lax
from jax.experimental import pallas as pl
from jax.experimental.pallas import tpu as pltpu
from jax.sharding import PartitionSpec as P

MOMENT = 0.95
COEFF_A = 3.4445
COEFF_B = -4.775
COEFF_C = 2.0315
EPSILON = 1e-07

F32, BF16, I32 = jnp.float32, jnp.bfloat16, jnp.int32
MESH = pl.DeviceIdType.MESH
D, FF, TOK, TOPK, CAP = 2048, 768, 64, 8, 16
PLANE, RING, SIDE = 16, 8, 4
PAIRS = TOK * TOPK
ROWS = 512
SPLIT = 2
CHUNK = ROWS // SPLIT
PIECE = CHUNK // 2
ORDER = (
    "P0", "G00", "G01", "G02", "B0", "B1", "P1", "G10", "G11", "G12", "I0", "M0", "M1", "I1",
    "E0", "E1", "W0", "I2", "F0", "A0", "S00", "B2", "P2", "G20", "G21", "G22", "W1", "F1",
    "A1", "S10", "S20", "B3", "M2", "W2", "A2", "S30", "M3", "E2", "P3", "G30", "G31", "G32",
    "S40", "E3", "F2", "S01", "W3", "A3", "S50", "F3", "S11", "S60", "S21", "S31", "S41", "S51",
    "S61",
)
BLK = 256
SPREAD = (
    ((1, 0), (-1, 0), (0, 1), (0, -1), (1, 1), (-1, -1), (1, -1), (-1, 1))
    + ((2, 0), (0, 2), (2, 1), (1, 2), (2, -1), (-1, 2), (2, 2))
)
PARTS = (((0, 0), (0, 1), (1, 1)), ((0, 2), (1, 2), (2, 2)))


def iota(shape, dim):
    return lax.broadcasted_iota(I32, shape, dim)


def dot(a, b):
    return jnp.dot(a, b, preferred_element_type=F32)


def kernel(
    act_hbm,
    og,
    gate,
    routes,
    mom_hbm,
    xs_out,
    mom_out,
    gram_out,
    act,
    mom,
    ogx,
    og_buf,
    a_send,
    a_buf,
    idx_mine,
    idx_peer,
    idx_send,
    idx_buf,
    sel,
    wt,
    first,
    ring,
    xs,
    gram_send,
    gram_core,
    gram_own,
    gram_sum,
    gram_z,
    gram_tot,
    local_sem,
    ogx_send,
    ogx_recv,
    og_send,
    og_recv,
    a_send_sem,
    a_recv_sem,
    a_own_sem,
    ap_send,
    ap_recv,
    idx_sems,
    idx_all_send,
    idx_all_recv,
    z_send,
    z_recv,
    g_send,
    g_recv,
):
    dp = lax.axis_index("dp")
    q = lax.axis_index("expert")
    z, c = lax.div(dp, 2), lax.rem(dp, 2)
    g0, zo = lax.div(z, 2), lax.rem(z, 2)
    qx, qy = lax.div(q, SIDE), lax.rem(q, SIDE)
    peer = 2 * z + 1 - c
    zr = 2 * lax.rem(z + 1, RING) + c
    zl = 2 * lax.rem(z + RING - 1, RING) + c
    zpair = 2 * (2 * g0 + 1 - zo) + c

    def send(src, dst, s_sem, r_sem, to_dp, to_q):
        copy = pltpu.make_async_remote_copy(
            src_ref=src,
            dst_ref=dst,
            send_sem=s_sem,
            recv_sem=r_sem,
            device_id=(to_dp, to_q),
            device_id_type=MESH,
        )
        copy.start()
        return copy

    pending = []
    mom_copy = pltpu.make_async_copy(mom_hbm, mom, local_sem.at[0])
    mom_copy.start()
    act_copy = pltpu.make_async_copy(act_hbm, act, local_sem.at[6])
    act_copy.start()

    barrier = pltpu.get_barrier_semaphore()

    def greet(i, carry):
        pl.semaphore_signal(
            barrier, inc=1, device_id=(dp, lax.rem(q + i, PLANE)), device_id_type=MESH
        )
        return carry

    lax.fori_loop(1, PLANE, greet, 0)
    for other in (peer, zr, zl):
        pl.semaphore_signal(barrier, inc=1, device_id=(other, q), device_id_type=MESH)
    pl.semaphore_wait(barrier, PLANE + 2)

    swaps, owns = [], []
    for o in range(2):
        zp = zo if o == 0 else 1 - zo
        mine = pl.multiple_of((2 * zp + c) * ROWS, ROWS)
        theirs = pl.multiple_of((2 * zp + 1 - c) * ROWS, ROWS)
        swaps.append(
            send(
                og.at[:, pl.ds(theirs, ROWS)],
                ogx.at[o, c],
                ogx_send.at[o],
                ogx_recv.at[o],
                peer,
                q,
            )
        )
        own = pltpu.make_async_copy(
            og.at[:, pl.ds(mine, ROWS)], ogx.at[o, c], local_sem.at[1 + o]
        )
        own.start()
        owns.append(own)

    spread = (lax.shift_right_logical(iota((TOK, PAIRS), 1), 3) == iota((TOK, PAIRS), 0)).astype(
        F32
    )
    own_k = (iota((TOPK, PAIRS), 1) & 7) == iota((TOPK, PAIRS), 0)

    def as_row(values):
        wide = jnp.dot(
            values, spread, precision=lax.Precision.HIGHEST, preferred_element_type=F32
        )
        return jnp.sum(jnp.where(own_k, wide, 0.0), axis=0, keepdims=True)

    route_row = as_row(routes[...].astype(F32))
    gate_row = as_row(gate[...])
    named = iota((TOK, PAIRS), 0).astype(F32) == route_row
    before = lax.shift_right_logical(iota((PAIRS, PAIRS), 0), 3) < lax.shift_right_logical(
        iota((PAIRS, PAIRS), 1), 3
    )
    counts = dot(named.astype(F32).astype(BF16), before.astype(F32).astype(BF16))
    place = jnp.sum(jnp.where(named, counts, 0.0), axis=0, keepdims=True)
    route_int = route_row.astype(I32)
    place_int = place.astype(I32)
    route_low, route_high = route_int & 3, lax.shift_right_logical(route_int, 2)
    slot = route_low * (PLANE * CAP) + route_high * CAP + place_int

    g_at = (
        lax.rem(g0 + 2, 4),
        lax.rem(g0 + 1 + 2 * zo, 4),
        lax.rem(g0 + 3 - 2 * zo, 4),
        g0,
    )

    u, v = (1 - c) * qx + c * qy, (1 - c) * qy + c * qx

    def at(du, dv):
        uu, vv = lax.rem(u + du + SIDE, SIDE), lax.rem(v + dv + SIDE, SIDE)
        return (1 - c) * (SIDE * uu + vv) + c * (SIDE * vv + uu)

    def pack(pos):
        if pos == 0:
            act_copy.wait()
        hit = (iota((PLANE * CAP, PAIRS), 0) + g_at[pos] * (PLANE * CAP)) == slot
        picked = dot(hit.astype(F32).astype(BF16), act[...])
        scale = jnp.sum(jnp.where(hit, gate_row, 0.0), axis=1, keepdims=True)
        a_send[pos] = (picked * scale).astype(BF16)

    def give(both):
        pos, third = both // 10, both % 10
        for du, dv in SPREAD[5 * third : 5 * third + 5]:
            to = at(du, dv)
            send(
                a_send.at[pos, pl.ds(pl.multiple_of(to * CAP, CAP), CAP)],
                a_buf.at[pos, qx, c, pl.ds(pl.multiple_of(qy * CAP, CAP), CAP)],
                a_send_sem.at[pos],
                a_recv_sem.at[pos],
                dp,
                to,
            )
        if third == 2:
            pltpu.make_async_copy(
                a_send.at[pos, pl.ds(pl.multiple_of(q * CAP, CAP), CAP)],
                a_buf.at[pos, qx, c, pl.ds(pl.multiple_of(qy * CAP, CAP), CAP)],
                a_own_sem.at[pos],
            ).start()

    def forward(pos):
        rest = a_send.at[pos, pl.ds(0, (PLANE - 1) * CAP)]
        pltpu.make_async_copy(rest, rest, a_recv_sem.at[pos]).wait()
        piece = a_send.at[pos, pl.ds(0, CAP)]
        pltpu.make_async_copy(piece, piece, a_own_sem.at[pos]).wait()
        copy = send(
            a_buf.at[pos, :, c], a_buf.at[pos, :, c], ap_send.at[pos], ap_recv.at[pos], peer, q
        )
        pending.append(copy)
        return copy

    def og_send_one(o, source, to, key):
        send(
            og_buf.at[o, source],
            og_buf.at[o, source],
            og_send.at[o],
            og_recv.at[o, key],
            dp,
            to,
        )

    def og_wait(o, source, key):
        pltpu.make_async_remote_copy(
            src_ref=og_buf.at[o, source],
            dst_ref=og_buf.at[o, source],
            send_sem=og_send.at[o],
            recv_sem=og_recv.at[o, key],
            device_id=(dp, q),
            device_id_type=MESH,
        ).wait_recv()

    k_du = (0, -1, 1, 2)

    def og_begin(o):
        if o < 2:
            swaps[o].wait_recv()
            owns[o].wait()
        cols = slice((o // 2) * CHUNK, (o // 2 + 1) * CHUNK)
        og_buf[o, q] = ogx[o % 2, :, :, cols].reshape(2 * TOK, CHUNK).T
        og_send_one(o, q, at(1, 0), 0)
        og_send_one(o, q, at(-1, 0), 1)
        og_send_one(o, q, at(0, 1), 3)
        og_send_one(o, q, at(0, -1), 7)

    def og_second(o, k):
        source = at(k_du[k], 0)
        og_send_one(o, source, at(0, 1), 3 + k)
        og_send_one(o, source, at(0, -1), 7 + k)

    def og_relay(o, k):
        if k < 2:
            og_wait(o, at(k_du[k], -1), 3 + k)
            og_send_one(o, at(k_du[k], -1), at(0, 1), 11 + k)
        else:
            og_wait(o, at(k_du[k], 1), 7 + k)
            og_send_one(o, at(k_du[k], 1), at(0, -1), 11 + k)

    def og_middle(o):
        og_wait(o, at(-1, 0), 0)
        if (o // 2 + o) % 2 == 0:
            og_send_one(o, at(-1, 0), at(1, 0), 2)
        og_second(o, 1)
        og_wait(o, at(1, 0), 1)
        if (o // 2 + o) % 2 == 1:
            og_send_one(o, at(1, 0), at(-1, 0), 2)
        og_second(o, 2)
        og_relay(o, 0)

    def og_end(o):
        og_wait(o, at(2, 0), 2)
        og_second(o, 3)
        for k in (1, 2, 3):
            og_relay(o, k)

    def og_all(o):
        for k in (2, 3):
            og_wait(o, at(k_du[k], -1), 3 + k)
        for k in (0, 1):
            og_wait(o, at(k_du[k], 1), 7 + k)
        for k in range(4):
            og_wait(o, at(k_du[k], 2), 11 + k)

    swapped = []

    def idx_begin():
        key_row = route_low * CAP + place_int
        token = lax.shift_right_logical(iota((TOK, PAIRS), 1), 3) + 1 + TOK * c
        key_hot = (
            jnp.where(iota((TOK, PAIRS), 0) == key_row, token, 0).astype(F32).astype(BF16)
        )
        high_hot = (iota((PLANE, PAIRS), 0) == route_high).astype(F32).astype(BF16)
        tokens = lax.dot_general(
            high_hot, key_hot, (((1,), (1,)), ((), ())), preferred_element_type=F32
        )
        lane = iota((TOK, PAIRS), 1)
        lane_key = lax.shift_right_logical(lane, 7) * CAP + (lane & 15)
        lane_mine = ((lax.shift_right_logical(lane, 6) & 1) == c) & (
            (lax.shift_right_logical(lane, 4) & 3) == qy
        )
        widen = (lane_mine & (lane_key == iota((TOK, PAIRS), 0))).astype(F32).astype(BF16)
        idx_mine[...] = dot(tokens.astype(BF16), widen)
        swapped.append(send(idx_mine, idx_peer, idx_sems.at[0], idx_sems.at[1], peer, q))

    def idx_share():
        swapped[0].wait_recv()
        both = idx_mine[...] + idx_peer[...]
        for i in range(PLANE):
            idx_send[i] = both[i : i + 1]

        def one(i, carry):
            to = lax.rem(q + i, PLANE)
            send(idx_send.at[to], idx_buf.at[q], idx_all_send.at[to], idx_all_recv.at[q], dp, to)
            return carry

        lax.fori_loop(1, PLANE, one, 0)
        idx_buf[q] = idx_send[q]

    def idx_end():
        def one(i, carry):
            source = lax.rem(q + i, PLANE)
            pltpu.make_async_copy(
                idx_buf.at[source], idx_buf.at[source], idx_all_recv.at[source]
            ).wait()
            return carry

        lax.fori_loop(1, PLANE, one, 0)
        for grp in range(4):
            for j in range(4):
                hit = (iota((2 * TOK, PAIRS), 0) + 1).astype(F32) == idx_buf[4 * grp + j]
                sel[grp, j * 128 : (j + 1) * 128] = hit.astype(F32).astype(BF16)

    def pick(o):
        rows = slice((o // 2) * CHUNK, (o // 2 + 1) * CHUNK)
        for grp in range(4):
            left = jnp.concatenate([og_buf[o, 4 * grp + j] for j in range(4)], axis=1)
            out = dot(left, sel[grp]).astype(BF16)
            for g in range(4):
                wt[g, o % 2, rows, grp * 128 : (grp + 1) * 128] = out[:, g * 128 : (g + 1) * 128]

    def partial(g, o, pos, low, n):
        cols = slice(n * BLK, (n + 1) * BLK)
        return dot(wt[g, o, low : low + PIECE], a_buf[pos, :, :, :, cols].reshape(PAIRS, BLK))

    def low_row(h, way, s):
        return s * CHUNK + PIECE * ((h + way) % 2)

    def step(h, s):
        dist = (4, 3, 3, 2, 2, 1, 1)[h]
        o = (0, 1, 1, 0, 0, 1, 1)[h]
        place_right = (0, 1 - zo, 1 - zo, 1 + zo, 1 + zo, 3 - zo, 3 - zo)[h]
        place_left = (0, zo, zo, 2 - zo, 2 - zo, 2 + zo, 2 + zo)[h]
        for way in range(2):
            dest = lax.rem(z + (dist if way == 0 else RING - dist), RING)
            g = lax.div(dest, 2)
            pos = place_right if way == 0 else place_left
            target = first.at[way, h, s] if h < 2 else ring.at[way, h - 2, s]
            if h >= 2:
                z_copies[way, h - 2, s].wait_recv()
            for n in range(3):
                cols = slice(n * BLK, (n + 1) * BLK)
                value = partial(g, o, pos, low_row(h, way, s), n)
                if h >= 2:
                    value = value + ring[way, h - 2, s, :, cols].astype(F32)
                target[:, cols] = value.astype(BF16)
            copy = send(
                target,
                ring.at[way, h, s],
                z_send.at[way, h, s],
                z_recv.at[way, h, s],
                zr if way == 0 else zl,
                q,
            )
            pending.append(copy)
            z_copies[way, h, s] = copy

    z_copies, arrive = {}, {}

    def og_final(o):
        og_all(o)
        pick(o)

    def pass_on(pos):
        arrive[pos] = forward(pos)

    def have(pos):
        arrive[pos].wait_recv()

    index = (idx_begin, idx_share, idx_end)
    work = {
        "P": pack,
        "G": give,
        "B": og_begin,
        "M": og_middle,
        "E": og_end,
        "F": og_final,
        "W": pass_on,
        "A": have,
        "I": lambda i: index[i](),
        "S": lambda both: step(both // 10, both % 10),
    }
    for name in ORDER:
        work[name[0]](int(name[1:]))

    def block_of(half, i, s):
        a, b = ((0, 2 * half), (half, 1 + half), (1 + half, 1 + half))[i]
        rows = slice(s * CHUNK, (s + 1) * CHUNK)
        return lax.dot_general(
            xs[rows, pl.ds(pl.multiple_of(a * BLK, BLK), BLK)],
            xs[rows, pl.ds(pl.multiple_of(b * BLK, BLK), BLK)],
            (((0,), (0,)), ((), ())),
            preferred_element_type=F32,
        )

    mom_copy.wait()
    for s in range(SPLIT):
        for way in range(2):
            z_copies[way, 5, s].wait_recv()
        for way in range(2):
            z_copies[way, 6, s].wait_recv()
        for odd in range(2):
            low = s * CHUNK + odd * PIECE
            rows = slice(low, low + PIECE)
            for n in range(3):
                cols = slice(n * BLK, (n + 1) * BLK)
                gradient = (
                    partial(g0, 0, 3, low, n)
                    + ring[0, 6 - odd, s, :, cols].astype(F32)
                    + ring[1, 5 + odd, s, :, cols].astype(F32)
                )
                momentum = MOMENT * mom[rows, cols] + gradient
                mom[rows, cols] = momentum
                xs[rows, cols] = (gradient + MOMENT * momentum).astype(BF16)
        if s < SPLIT - 1:
            for half in range(2):
                for i in range(3):
                    value = block_of(half, i, s)
                    gram_own[half, i] = value if s == 0 else gram_own[half, i] + value
    to_core, to_z, back = [], [], []
    for i in range(3):
        gram_send[i] = (gram_own[1 - c, i] + block_of(1 - c, i, SPLIT - 1)).astype(BF16)
        to_core.append(
            send(gram_send.at[i], gram_core.at[i], g_send.at[0, i], g_recv.at[0, i], peer, q)
        )
    for i in range(3):
        gram_own[c, i] = gram_own[c, i] + block_of(c, i, SPLIT - 1)
    outs = [
        pltpu.make_async_copy(xs, xs_out, local_sem.at[3]),
        pltpu.make_async_copy(mom, mom_out, local_sem.at[4]),
    ]
    for copy in outs:
        copy.start()
    for i in range(3):
        to_core[i].wait_recv()
        gram_sum[i] = (gram_own[c, i] + gram_core[i].astype(F32)).astype(BF16)
        to_z.append(
            send(gram_sum.at[i], gram_z.at[i], g_send.at[1, i], g_recv.at[1, i], zpair, q)
        )
    for i in range(3):
        to_z[i].wait_recv()
        gram_tot[c, i] = (gram_sum[i].astype(F32) + gram_z[i].astype(F32)).astype(BF16)
        back.append(
            send(
                gram_tot.at[c, i],
                gram_tot.at[c, i],
                g_send.at[2, i],
                g_recv.at[2, i],
                peer,
                q,
            )
        )
    for copy in back:
        copy.wait_recv()
    copy = pltpu.make_async_copy(gram_tot, gram_out, local_sem.at[5])
    copy.start()
    outs.append(copy)

    for copy in swaps + swapped + pending + to_core + to_z + back:
        copy.wait_send()
    for copy in outs:
        copy.wait()
    for pos in range(4):
        rest = a_send.at[pos, pl.ds(0, (PLANE - 1) * CAP)]
        pltpu.make_async_copy(rest, rest, a_send_sem.at[pos]).wait()

    for o in range(2 * SPLIT):
        rest = og_buf.at[o, pl.ds(0, PLANE - 1)]
        pltpu.make_async_copy(rest, rest, og_send.at[o]).wait()

    def idx_done(i, carry):
        to = lax.rem(q + i, PLANE)
        pltpu.make_async_copy(idx_send.at[to], idx_send.at[to], idx_all_send.at[to]).wait()
        return carry

    lax.fori_loop(1, PLANE, idx_done, 0)


def newton(
    xs_hbm, gram_hbm, mom_hbm, update, new_mom, xs, gram_tot, gram, poly, hmat, hmat16, x1, mom, sem
):
    gram_copy = pltpu.make_async_copy(gram_hbm, gram_tot, sem.at[1])
    gram_copy.start()
    xs_copy = pltpu.make_async_copy(xs_hbm, xs, sem.at[2])
    xs_copy.start()
    mom_copy = pltpu.make_async_copy(mom_hbm, mom, sem.at[0])
    mom_copy.start()
    gram_copy.wait()
    trace = jnp.zeros((1, 1), F32)
    eye = iota((BLK, BLK), 0) == iota((BLK, BLK), 1)
    for half in range(2):
        for i, (a, b) in enumerate(PARTS[half]):
            block = gram_tot[half, i]
            gram[a * BLK : (a + 1) * BLK, b * BLK : (b + 1) * BLK] = block
            wide = block.astype(F32)
            if a == b:
                trace = trace + jnp.sum(
                    jnp.sum(jnp.where(eye, wide, 0.0), axis=1, keepdims=True), axis=0, keepdims=True
                )
            else:
                gram[b * BLK : (b + 1) * BLK, a * BLK : (a + 1) * BLK] = wide.T.astype(BF16)
    scale = 1.0 / (jnp.sqrt(trace) + EPSILON)
    scale2 = scale * scale

    def rows_of(t):
        return slice(t * BLK, (t + 1) * BLK)

    for t in range(3):
        square = dot(gram[rows_of(t)], gram[...])
        poly[rows_of(t)] = (
            (COEFF_B * scale2) * gram[rows_of(t)].astype(F32)
            + (COEFF_C * scale2 * scale2) * square
        ).astype(BF16)
    for t in range(3):
        value = scale2 * (
            COEFF_A * gram[rows_of(t)].astype(F32) + dot(poly[rows_of(t)], gram[...])
        )
        hmat[rows_of(t)] = value
        hmat16[rows_of(t)] = value.astype(BF16)
    mom_copy.wait()
    mom_back = pltpu.make_async_copy(mom, new_mom, sem.at[0])
    mom_back.start()
    xs_copy.wait()
    for t in range(2):
        value = COEFF_A * xs[rows_of(t)].astype(F32) + dot(xs[rows_of(t)], poly[...])
        x1[rows_of(t)] = (scale * value).astype(BF16)
    for t in range(3):
        value = COEFF_A * hmat[rows_of(t)] + dot(hmat16[rows_of(t)], poly[...])
        gram[rows_of(t)] = value.astype(BF16)
    for t in range(3):
        square = dot(gram[rows_of(t)], gram[...])
        hmat16[rows_of(t)] = (
            COEFF_B * gram[rows_of(t)].astype(F32) + COEFF_C * square
        ).astype(BF16)
    for t in range(2):
        value = COEFF_A * x1[rows_of(t)].astype(F32) + dot(x1[rows_of(t)], hmat16[...])
        update[rows_of(t)] = (math.sqrt(D) * value.astype(BF16).astype(F32)).astype(BF16)

    mom_back.wait()


def body(activations, out_grad, gate_weights, routes, momentum):
    vmem = pl.BlockSpec(memory_space=pltpu.VMEM)
    dma = pltpu.SemaphoreType.DMA
    scratch = [
        pltpu.VMEM((PAIRS, FF), BF16),
        pltpu.VMEM((ROWS, FF), F32),
        pltpu.VMEM((2, 2, TOK, ROWS), BF16),
        pltpu.VMEM((2 * SPLIT, PLANE, CHUNK, 2 * TOK), BF16),
        pltpu.VMEM((4, PLANE * CAP, FF), BF16),
        pltpu.VMEM((4, 4, 2, 4 * CAP, FF), BF16),
        pltpu.VMEM((PLANE, PAIRS), F32),
        pltpu.VMEM((PLANE, PAIRS), F32),
        pltpu.VMEM((PLANE, 1, PAIRS), F32),
        pltpu.VMEM((PLANE, 1, PAIRS), F32),
        pltpu.VMEM((4, PAIRS, PAIRS), BF16),
        pltpu.VMEM((4, 2, ROWS, PAIRS), BF16),
        pltpu.VMEM((2, 2, SPLIT, PIECE, FF), BF16),
        pltpu.VMEM((2, 7, SPLIT, PIECE, FF), BF16),
        pltpu.VMEM((ROWS, FF), BF16),
        pltpu.VMEM((3, BLK, BLK), BF16),
        pltpu.VMEM((3, BLK, BLK), BF16),
        pltpu.VMEM((2, 3, BLK, BLK), F32),
        pltpu.VMEM((3, BLK, BLK), BF16),
        pltpu.VMEM((3, BLK, BLK), BF16),
        pltpu.VMEM((2, 3, BLK, BLK), BF16),
        dma((7,)),
        dma((2,)),
        dma((2,)),
        dma((2 * SPLIT,)),
        dma((2 * SPLIT, 15)),
        dma((4,)),
        dma((4,)),
        dma((4,)),
        dma((4,)),
        dma((4,)),
        dma((2,)),
        dma((PLANE,)),
        dma((PLANE,)),
        dma((2, 7, SPLIT)),
        dma((2, 7, SPLIT)),
        dma((3, 3)),
        dma((3, 3)),
    ]
    hbm = pl.BlockSpec(memory_space=pltpu.HBM)
    xs, moved, gram_tot = pl.pallas_call(
        kernel,
        out_shape=(
            jax.ShapeDtypeStruct((ROWS, FF), BF16),
            jax.ShapeDtypeStruct((ROWS, FF), F32),
            jax.ShapeDtypeStruct((2, 3, BLK, BLK), BF16),
        ),
        in_specs=[hbm, hbm, vmem, vmem, hbm],
        out_specs=(hbm, hbm, hbm),
        scratch_shapes=scratch,
        compiler_params=pltpu.CompilerParams(
            collective_id=0, has_side_effects=True, vmem_limit_bytes=60 * 2**20
        ),
    )(activations.reshape(PAIRS, FF), out_grad, gate_weights.T, routes.T, momentum)
    return pl.pallas_call(
        newton,
        out_shape=(
            jax.ShapeDtypeStruct((ROWS, FF), BF16),
            jax.ShapeDtypeStruct((ROWS, FF), F32),
        ),
        in_specs=[hbm, hbm, hbm],
        out_specs=(vmem, hbm),
        scratch_shapes=[
            pltpu.VMEM((ROWS, FF), BF16),
            pltpu.VMEM((2, 3, BLK, BLK), BF16),
            pltpu.VMEM((FF, FF), BF16),
            pltpu.VMEM((FF, FF), BF16),
            pltpu.VMEM((FF, FF), F32),
            pltpu.VMEM((FF, FF), BF16),
            pltpu.VMEM((ROWS, FF), BF16),
            pltpu.VMEM((ROWS, FF), F32),
            dma((3,)),
        ],
        compiler_params=pltpu.CompilerParams(vmem_limit_bytes=60 * 2**20),
    )(xs, gram_tot, moved)


def solution(mesh):
    in_specs = (
        P(("dp", "expert"), None, None),
        P(("dp", "expert"), None),
        P(("dp", "expert"), None),
        P(("dp", "expert"), None),
        P(("expert", "dp"), None),
    )
    out_specs = (P(("expert", "dp"), None), P(("expert", "dp"), None))
    return jax.shard_map(body, mesh=mesh, in_specs=in_specs, out_specs=out_specs, check_vma=False)
```

```python
import math

import jax
import jax.numpy as jnp
from jax import lax
from jax.experimental import pallas as pl
from jax.experimental.pallas import tpu as pltpu
from jax.sharding import PartitionSpec as P

MOMENT = 0.95
COEFF_A = 3.4445
COEFF_B = -4.775
COEFF_C = 2.0315
EPSILON = 1e-07

F32, BF16, I32 = jnp.float32, jnp.bfloat16, jnp.int32
MESH = pl.DeviceIdType.MESH
D, FF, TOK, TOPK, CAP = 2048, 768, 64, 8, 16
PLANE, RING, SIDE = 16, 8, 4
PAIRS = TOK * TOPK
ROWS = 512
SPLIT = 2
CHUNK = ROWS // SPLIT
PIECE = CHUNK // 2
ORDER = (
    "B0", "P0", "G00", "G01", "G02", "B1", "I0", "M0", "I1", "M1", "E0", "W0", "P1", "G10",
    "G11", "G12", "I2", "E1", "P2", "G20", "G21", "G22", "F0", "A0", "S00", "W1", "P3", "G30",
    "G31", "G32", "B2", "F1", "A1", "S10", "S20", "B3", "M2", "W2", "A2", "S30", "M3", "E2",
    "W3", "S40", "E3", "A3", "F2", "S50", "S01", "S60", "F3", "S11", "S21", "S31", "S41", "S51",
    "S61",
)
BLK = 256
SPREAD = (
    ((1, 0), (-1, 0), (0, 1), (0, -1), (1, 1), (-1, -1), (1, -1), (-1, 1))
    + ((2, 0), (0, 2), (2, 1), (1, 2), (2, -1), (-1, 2), (2, 2))
)
PARTS = (((0, 0), (0, 1), (1, 1)), ((0, 2), (1, 2), (2, 2)))


def iota(shape, dim):
    return lax.broadcasted_iota(I32, shape, dim)


def dot(a, b):
    return jnp.dot(a, b, preferred_element_type=F32)


def kernel(
    act_hbm,
    og,
    gate,
    routes,
    mom_hbm,
    xs_out,
    mom_out,
    gram_out,
    act,
    mom,
    ogx,
    og_buf,
    a_send,
    a_buf,
    idx_mine,
    idx_peer,
    idx_send,
    idx_buf,
    sel,
    wt,
    first,
    ring,
    xs,
    gram_send,
    gram_core,
    gram_own,
    gram_sum,
    gram_z,
    gram_tot,
    local_sem,
    ogx_send,
    ogx_recv,
    og_send,
    og_recv,
    a_send_sem,
    a_recv_sem,
    a_own_sem,
    ap_send,
    ap_recv,
    idx_sems,
    idx_all_send,
    idx_all_recv,
    z_send,
    z_recv,
    g_send,
    g_recv,
):
    dp = lax.axis_index("dp")
    q = lax.axis_index("expert")
    z, c = lax.div(dp, 2), lax.rem(dp, 2)
    g0, zo = lax.div(z, 2), lax.rem(z, 2)
    qx, qy = lax.div(q, SIDE), lax.rem(q, SIDE)
    peer = 2 * z + 1 - c
    zr = 2 * lax.rem(z + 1, RING) + c
    zl = 2 * lax.rem(z + RING - 1, RING) + c
    zpair = 2 * (2 * g0 + 1 - zo) + c

    def send(src, dst, s_sem, r_sem, to_dp, to_q):
        copy = pltpu.make_async_remote_copy(
            src_ref=src,
            dst_ref=dst,
            send_sem=s_sem,
            recv_sem=r_sem,
            device_id=(to_dp, to_q),
            device_id_type=MESH,
        )
        copy.start()
        return copy

    pending = []
    mom_copy = pltpu.make_async_copy(mom_hbm, mom, local_sem.at[0])
    mom_copy.start()
    act_copy = pltpu.make_async_copy(act_hbm, act, local_sem.at[6])
    act_copy.start()

    barrier = pltpu.get_barrier_semaphore()

    def greet(i, carry):
        pl.semaphore_signal(
            barrier, inc=1, device_id=(dp, lax.rem(q + i, PLANE)), device_id_type=MESH
        )
        return carry

    lax.fori_loop(1, PLANE, greet, 0)
    for other in (peer, zr, zl):
        pl.semaphore_signal(barrier, inc=1, device_id=(other, q), device_id_type=MESH)
    pl.semaphore_wait(barrier, PLANE + 2)

    swaps, owns = [], []
    for o in range(2):
        zp = zo if o == 0 else 1 - zo
        mine = pl.multiple_of((2 * zp + c) * ROWS, ROWS)
        theirs = pl.multiple_of((2 * zp + 1 - c) * ROWS, ROWS)
        swaps.append(
            send(
                og.at[:, pl.ds(theirs, ROWS)],
                ogx.at[o, c],
                ogx_send.at[o],
                ogx_recv.at[o],
                peer,
                q,
            )
        )
        own = pltpu.make_async_copy(
            og.at[:, pl.ds(mine, ROWS)], ogx.at[o, c], local_sem.at[1 + o]
        )
        own.start()
        owns.append(own)

    spread = (lax.shift_right_logical(iota((TOK, PAIRS), 1), 3) == iota((TOK, PAIRS), 0)).astype(
        F32
    )
    own_k = (iota((TOPK, PAIRS), 1) & 7) == iota((TOPK, PAIRS), 0)

    def as_row(values):
        wide = jnp.dot(
            values, spread, precision=lax.Precision.HIGHEST, preferred_element_type=F32
        )
        return jnp.sum(jnp.where(own_k, wide, 0.0), axis=0, keepdims=True)

    route_row = as_row(routes[...].astype(F32))
    gate_row = as_row(gate[...])
    named = iota((TOK, PAIRS), 0).astype(F32) == route_row
    before = lax.shift_right_logical(iota((PAIRS, PAIRS), 0), 3) < lax.shift_right_logical(
        iota((PAIRS, PAIRS), 1), 3
    )
    counts = dot(named.astype(F32).astype(BF16), before.astype(F32).astype(BF16))
    place = jnp.sum(jnp.where(named, counts, 0.0), axis=0, keepdims=True)
    route_int = route_row.astype(I32)
    place_int = place.astype(I32)
    route_low, route_high = route_int & 3, lax.shift_right_logical(route_int, 2)
    slot = route_low * (PLANE * CAP) + route_high * CAP + place_int

    g_at = (
        lax.rem(g0 + 2, 4),
        lax.rem(g0 + 1 + 2 * zo, 4),
        lax.rem(g0 + 3 - 2 * zo, 4),
        g0,
    )

    u, v = (1 - c) * qx + c * qy, (1 - c) * qy + c * qx

    def at(du, dv):
        uu, vv = lax.rem(u + du + SIDE, SIDE), lax.rem(v + dv + SIDE, SIDE)
        return (1 - c) * (SIDE * uu + vv) + c * (SIDE * vv + uu)

    def pack(pos):
        if pos == 0:
            act_copy.wait()
        hit = (iota((PLANE * CAP, PAIRS), 0) + g_at[pos] * (PLANE * CAP)) == slot
        picked = dot(hit.astype(F32).astype(BF16), act[...])
        scale = jnp.sum(jnp.where(hit, gate_row, 0.0), axis=1, keepdims=True)
        a_send[pos] = (picked * scale).astype(BF16)

    def give(both):
        pos, third = both // 10, both % 10
        for du, dv in SPREAD[5 * third : 5 * third + 5]:
            to = at(du, dv)
            send(
                a_send.at[pos, pl.ds(pl.multiple_of(to * CAP, CAP), CAP)],
                a_buf.at[pos, qx, c, pl.ds(pl.multiple_of(qy * CAP, CAP), CAP)],
                a_send_sem.at[pos],
                a_recv_sem.at[pos],
                dp,
                to,
            )
        if third == 2:
            pltpu.make_async_copy(
                a_send.at[pos, pl.ds(pl.multiple_of(q * CAP, CAP), CAP)],
                a_buf.at[pos, qx, c, pl.ds(pl.multiple_of(qy * CAP, CAP), CAP)],
                a_own_sem.at[pos],
            ).start()

    def forward(pos):
        rest = a_send.at[pos, pl.ds(0, (PLANE - 1) * CAP)]
        pltpu.make_async_copy(rest, rest, a_recv_sem.at[pos]).wait()
        piece = a_send.at[pos, pl.ds(0, CAP)]
        pltpu.make_async_copy(piece, piece, a_own_sem.at[pos]).wait()
        copy = send(
            a_buf.at[pos, :, c], a_buf.at[pos, :, c], ap_send.at[pos], ap_recv.at[pos], peer, q
        )
        pending.append(copy)
        return copy

    def og_send_one(o, source, to, key):
        send(
            og_buf.at[o, source],
            og_buf.at[o, source],
            og_send.at[o],
            og_recv.at[o, key],
            dp,
            to,
        )

    def og_wait(o, source, key):
        pltpu.make_async_remote_copy(
            src_ref=og_buf.at[o, source],
            dst_ref=og_buf.at[o, source],
            send_sem=og_send.at[o],
            recv_sem=og_recv.at[o, key],
            device_id=(dp, q),
            device_id_type=MESH,
        ).wait_recv()

    k_du = (0, -1, 1, 2)

    def og_begin(o):
        if o < 2:
            swaps[o].wait_recv()
            owns[o].wait()
        cols = slice((o // 2) * CHUNK, (o // 2 + 1) * CHUNK)
        og_buf[o, q] = ogx[o % 2, :, :, cols].reshape(2 * TOK, CHUNK).T
        og_send_one(o, q, at(1, 0), 0)
        og_send_one(o, q, at(-1, 0), 1)
        og_send_one(o, q, at(0, 1), 3)
        og_send_one(o, q, at(0, -1), 7)

    def og_second(o, k):
        source = at(k_du[k], 0)
        og_send_one(o, source, at(0, 1), 3 + k)
        og_send_one(o, source, at(0, -1), 7 + k)

    def og_relay(o, k):
        if k < 2:
            og_wait(o, at(k_du[k], -1), 3 + k)
            og_send_one(o, at(k_du[k], -1), at(0, 1), 11 + k)
        else:
            og_wait(o, at(k_du[k], 1), 7 + k)
            og_send_one(o, at(k_du[k], 1), at(0, -1), 11 + k)

    def og_middle(o):
        og_wait(o, at(-1, 0), 0)
        if (o // 2 + o) % 2 == 0:
            og_send_one(o, at(-1, 0), at(1, 0), 2)
        og_second(o, 1)
        og_wait(o, at(1, 0), 1)
        if (o // 2 + o) % 2 == 1:
            og_send_one(o, at(1, 0), at(-1, 0), 2)
        og_second(o, 2)
        og_relay(o, 0)

    def og_end(o):
        og_wait(o, at(2, 0), 2)
        og_second(o, 3)
        for k in (1, 2, 3):
            og_relay(o, k)

    def og_all(o):
        for k in (2, 3):
            og_wait(o, at(k_du[k], -1), 3 + k)
        for k in (0, 1):
            og_wait(o, at(k_du[k], 1), 7 + k)
        for k in range(4):
            og_wait(o, at(k_du[k], 2), 11 + k)

    swapped = []

    def idx_begin():
        key_row = route_low * CAP + place_int
        token = lax.shift_right_logical(iota((TOK, PAIRS), 1), 3) + 1 + TOK * c
        key_hot = (
            jnp.where(iota((TOK, PAIRS), 0) == key_row, token, 0).astype(F32).astype(BF16)
        )
        high_hot = (iota((PLANE, PAIRS), 0) == route_high).astype(F32).astype(BF16)
        tokens = lax.dot_general(
            high_hot, key_hot, (((1,), (1,)), ((), ())), preferred_element_type=F32
        )
        lane = iota((TOK, PAIRS), 1)
        lane_key = lax.shift_right_logical(lane, 7) * CAP + (lane & 15)
        lane_mine = ((lax.shift_right_logical(lane, 6) & 1) == c) & (
            (lax.shift_right_logical(lane, 4) & 3) == qy
        )
        widen = (lane_mine & (lane_key == iota((TOK, PAIRS), 0))).astype(F32).astype(BF16)
        idx_mine[...] = dot(tokens.astype(BF16), widen)
        swapped.append(send(idx_mine, idx_peer, idx_sems.at[0], idx_sems.at[1], peer, q))

    def idx_share():
        swapped[0].wait_recv()
        both = idx_mine[...] + idx_peer[...]
        for i in range(PLANE):
            idx_send[i] = both[i : i + 1]

        def one(i, carry):
            to = lax.rem(q + i, PLANE)
            send(idx_send.at[to], idx_buf.at[q], idx_all_send.at[to], idx_all_recv.at[q], dp, to)
            return carry

        lax.fori_loop(1, PLANE, one, 0)
        idx_buf[q] = idx_send[q]

    def idx_end():
        def one(i, carry):
            source = lax.rem(q + i, PLANE)
            pltpu.make_async_copy(
                idx_buf.at[source], idx_buf.at[source], idx_all_recv.at[source]
            ).wait()
            return carry

        lax.fori_loop(1, PLANE, one, 0)
        for grp in range(4):
            for j in range(4):
                hit = (iota((2 * TOK, PAIRS), 0) + 1).astype(F32) == idx_buf[4 * grp + j]
                sel[grp, j * 128 : (j + 1) * 128] = hit.astype(F32).astype(BF16)

    def pick(o):
        rows = slice((o // 2) * CHUNK, (o // 2 + 1) * CHUNK)
        for grp in range(4):
            left = jnp.concatenate([og_buf[o, 4 * grp + j] for j in range(4)], axis=1)
            out = dot(left, sel[grp]).astype(BF16)
            for g in range(4):
                wt[g, o % 2, rows, grp * 128 : (grp + 1) * 128] = out[:, g * 128 : (g + 1) * 128]

    def partial(g, o, pos, low, n):
        cols = slice(n * BLK, (n + 1) * BLK)
        return dot(wt[g, o, low : low + PIECE], a_buf[pos, :, :, :, cols].reshape(PAIRS, BLK))

    def low_row(h, way, s):
        return s * CHUNK + PIECE * ((h + way) % 2)

    def step(h, s):
        dist = (4, 3, 3, 2, 2, 1, 1)[h]
        o = (0, 1, 1, 0, 0, 1, 1)[h]
        place_right = (0, 1 - zo, 1 - zo, 1 + zo, 1 + zo, 3 - zo, 3 - zo)[h]
        place_left = (0, zo, zo, 2 - zo, 2 - zo, 2 + zo, 2 + zo)[h]
        for way in range(2):
            dest = lax.rem(z + (dist if way == 0 else RING - dist), RING)
            g = lax.div(dest, 2)
            pos = place_right if way == 0 else place_left
            target = first.at[way, h, s] if h < 2 else ring.at[way, h - 2, s]
            if h >= 2:
                z_copies[way, h - 2, s].wait_recv()
            for n in range(3):
                cols = slice(n * BLK, (n + 1) * BLK)
                value = partial(g, o, pos, low_row(h, way, s), n)
                if h >= 2:
                    value = value + ring[way, h - 2, s, :, cols].astype(F32)
                target[:, cols] = value.astype(BF16)
            copy = send(
                target,
                ring.at[way, h, s],
                z_send.at[way, h, s],
                z_recv.at[way, h, s],
                zr if way == 0 else zl,
                q,
            )
            pending.append(copy)
            z_copies[way, h, s] = copy

    z_copies, arrive = {}, {}

    def og_final(o):
        og_all(o)
        pick(o)

    def pass_on(pos):
        arrive[pos] = forward(pos)

    def have(pos):
        arrive[pos].wait_recv()

    index = (idx_begin, idx_share, idx_end)
    work = {
        "P": pack,
        "G": give,
        "B": og_begin,
        "M": og_middle,
        "E": og_end,
        "F": og_final,
        "W": pass_on,
        "A": have,
        "I": lambda i: index[i](),
        "S": lambda both: step(both // 10, both % 10),
    }
    for name in ORDER:
        work[name[0]](int(name[1:]))

    def block_of(half, i, s):
        a, b = ((0, 2 * half), (half, 1 + half), (1 + half, 1 + half))[i]
        rows = slice(s * CHUNK, (s + 1) * CHUNK)
        return lax.dot_general(
            xs[rows, pl.ds(pl.multiple_of(a * BLK, BLK), BLK)],
            xs[rows, pl.ds(pl.multiple_of(b * BLK, BLK), BLK)],
            (((0,), (0,)), ((), ())),
            preferred_element_type=F32,
        )

    mom_copy.wait()
    for s in range(SPLIT):
        for way in range(2):
            z_copies[way, 5, s].wait_recv()
        for way in range(2):
            z_copies[way, 6, s].wait_recv()
        for odd in range(2):
            low = s * CHUNK + odd * PIECE
            rows = slice(low, low + PIECE)
            for n in range(3):
                cols = slice(n * BLK, (n + 1) * BLK)
                gradient = (
                    partial(g0, 0, 3, low, n)
                    + ring[0, 6 - odd, s, :, cols].astype(F32)
                    + ring[1, 5 + odd, s, :, cols].astype(F32)
                )
                momentum = MOMENT * mom[rows, cols] + gradient
                mom[rows, cols] = momentum
                xs[rows, cols] = (gradient + MOMENT * momentum).astype(BF16)
        if s < SPLIT - 1:
            for half in range(2):
                for i in range(3):
                    value = block_of(half, i, s)
                    gram_own[half, i] = value if s == 0 else gram_own[half, i] + value
    to_core, to_z, back = [], [], []
    for i in range(3):
        gram_send[i] = (gram_own[1 - c, i] + block_of(1 - c, i, SPLIT - 1)).astype(BF16)
        to_core.append(
            send(gram_send.at[i], gram_core.at[i], g_send.at[0, i], g_recv.at[0, i], peer, q)
        )
    for i in range(3):
        gram_own[c, i] = gram_own[c, i] + block_of(c, i, SPLIT - 1)
    outs = [
        pltpu.make_async_copy(xs, xs_out, local_sem.at[3]),
        pltpu.make_async_copy(mom, mom_out, local_sem.at[4]),
    ]
    for copy in outs:
        copy.start()
    for i in range(3):
        to_core[i].wait_recv()
        gram_sum[i] = (gram_own[c, i] + gram_core[i].astype(F32)).astype(BF16)
        to_z.append(
            send(gram_sum.at[i], gram_z.at[i], g_send.at[1, i], g_recv.at[1, i], zpair, q)
        )
    for i in range(3):
        to_z[i].wait_recv()
        gram_tot[c, i] = (gram_sum[i].astype(F32) + gram_z[i].astype(F32)).astype(BF16)
        back.append(
            send(
                gram_tot.at[c, i],
                gram_tot.at[c, i],
                g_send.at[2, i],
                g_recv.at[2, i],
                peer,
                q,
            )
        )
    for copy in back:
        copy.wait_recv()
    copy = pltpu.make_async_copy(gram_tot, gram_out, local_sem.at[5])
    copy.start()
    outs.append(copy)

    for copy in swaps + swapped + pending + to_core + to_z + back:
        copy.wait_send()
    for copy in outs:
        copy.wait()
    for pos in range(4):
        rest = a_send.at[pos, pl.ds(0, (PLANE - 1) * CAP)]
        pltpu.make_async_copy(rest, rest, a_send_sem.at[pos]).wait()

    for o in range(2 * SPLIT):
        rest = og_buf.at[o, pl.ds(0, PLANE - 1)]
        pltpu.make_async_copy(rest, rest, og_send.at[o]).wait()

    def idx_done(i, carry):
        to = lax.rem(q + i, PLANE)
        pltpu.make_async_copy(idx_send.at[to], idx_send.at[to], idx_all_send.at[to]).wait()
        return carry

    lax.fori_loop(1, PLANE, idx_done, 0)


def newton(
    xs_hbm, gram_hbm, mom_hbm, update, new_mom, xs, gram_tot, gram, poly, hmat, hmat16, x1, mom, sem
):
    gram_copy = pltpu.make_async_copy(gram_hbm, gram_tot, sem.at[1])
    gram_copy.start()
    xs_copy = pltpu.make_async_copy(xs_hbm, xs, sem.at[2])
    xs_copy.start()
    mom_copy = pltpu.make_async_copy(mom_hbm, mom, sem.at[0])
    mom_copy.start()
    gram_copy.wait()
    trace = jnp.zeros((1, 1), F32)
    eye = iota((BLK, BLK), 0) == iota((BLK, BLK), 1)
    for half in range(2):
        for i, (a, b) in enumerate(PARTS[half]):
            block = gram_tot[half, i]
            gram[a * BLK : (a + 1) * BLK, b * BLK : (b + 1) * BLK] = block
            wide = block.astype(F32)
            if a == b:
                trace = trace + jnp.sum(
                    jnp.sum(jnp.where(eye, wide, 0.0), axis=1, keepdims=True), axis=0, keepdims=True
                )
            else:
                gram[b * BLK : (b + 1) * BLK, a * BLK : (a + 1) * BLK] = wide.T.astype(BF16)
    scale = 1.0 / (jnp.sqrt(trace) + EPSILON)
    scale2 = scale * scale

    def rows_of(t):
        return slice(t * BLK, (t + 1) * BLK)

    for t in range(3):
        square = dot(gram[rows_of(t)], gram[...])
        poly[rows_of(t)] = (
            (COEFF_B * scale2) * gram[rows_of(t)].astype(F32)
            + (COEFF_C * scale2 * scale2) * square
        ).astype(BF16)
    for t in range(3):
        value = scale2 * (
            COEFF_A * gram[rows_of(t)].astype(F32) + dot(poly[rows_of(t)], gram[...])
        )
        hmat[rows_of(t)] = value
        hmat16[rows_of(t)] = value.astype(BF16)
    mom_copy.wait()
    mom_back = pltpu.make_async_copy(mom, new_mom, sem.at[0])
    mom_back.start()
    xs_copy.wait()
    for t in range(2):
        value = COEFF_A * xs[rows_of(t)].astype(F32) + dot(xs[rows_of(t)], poly[...])
        x1[rows_of(t)] = (scale * value).astype(BF16)
    for t in range(3):
        value = COEFF_A * hmat[rows_of(t)] + dot(hmat16[rows_of(t)], poly[...])
        gram[rows_of(t)] = value.astype(BF16)
    for t in range(3):
        square = dot(gram[rows_of(t)], gram[...])
        hmat16[rows_of(t)] = (
            COEFF_B * gram[rows_of(t)].astype(F32) + COEFF_C * square
        ).astype(BF16)
    for t in range(2):
        value = COEFF_A * x1[rows_of(t)].astype(F32) + dot(x1[rows_of(t)], hmat16[...])
        update[rows_of(t)] = (math.sqrt(D) * value.astype(BF16).astype(F32)).astype(BF16)

    mom_back.wait()


def body(activations, out_grad, gate_weights, routes, momentum):
    vmem = pl.BlockSpec(memory_space=pltpu.VMEM)
    dma = pltpu.SemaphoreType.DMA
    scratch = [
        pltpu.VMEM((PAIRS, FF), BF16),
        pltpu.VMEM((ROWS, FF), F32),
        pltpu.VMEM((2, 2, TOK, ROWS), BF16),
        pltpu.VMEM((2 * SPLIT, PLANE, CHUNK, 2 * TOK), BF16),
        pltpu.VMEM((4, PLANE * CAP, FF), BF16),
        pltpu.VMEM((4, 4, 2, 4 * CAP, FF), BF16),
        pltpu.VMEM((PLANE, PAIRS), F32),
        pltpu.VMEM((PLANE, PAIRS), F32),
        pltpu.VMEM((PLANE, 1, PAIRS), F32),
        pltpu.VMEM((PLANE, 1, PAIRS), F32),
        pltpu.VMEM((4, PAIRS, PAIRS), BF16),
        pltpu.VMEM((4, 2, ROWS, PAIRS), BF16),
        pltpu.VMEM((2, 2, SPLIT, PIECE, FF), BF16),
        pltpu.VMEM((2, 7, SPLIT, PIECE, FF), BF16),
        pltpu.VMEM((ROWS, FF), BF16),
        pltpu.VMEM((3, BLK, BLK), BF16),
        pltpu.VMEM((3, BLK, BLK), BF16),
        pltpu.VMEM((2, 3, BLK, BLK), F32),
        pltpu.VMEM((3, BLK, BLK), BF16),
        pltpu.VMEM((3, BLK, BLK), BF16),
        pltpu.VMEM((2, 3, BLK, BLK), BF16),
        dma((7,)),
        dma((2,)),
        dma((2,)),
        dma((2 * SPLIT,)),
        dma((2 * SPLIT, 15)),
        dma((4,)),
        dma((4,)),
        dma((4,)),
        dma((4,)),
        dma((4,)),
        dma((2,)),
        dma((PLANE,)),
        dma((PLANE,)),
        dma((2, 7, SPLIT)),
        dma((2, 7, SPLIT)),
        dma((3, 3)),
        dma((3, 3)),
    ]
    hbm = pl.BlockSpec(memory_space=pltpu.HBM)
    xs, moved, gram_tot = pl.pallas_call(
        kernel,
        out_shape=(
            jax.ShapeDtypeStruct((ROWS, FF), BF16),
            jax.ShapeDtypeStruct((ROWS, FF), F32),
            jax.ShapeDtypeStruct((2, 3, BLK, BLK), BF16),
        ),
        in_specs=[hbm, hbm, vmem, vmem, hbm],
        out_specs=(hbm, hbm, hbm),
        scratch_shapes=scratch,
        compiler_params=pltpu.CompilerParams(
            collective_id=0, has_side_effects=True, vmem_limit_bytes=60 * 2**20
        ),
    )(activations.reshape(PAIRS, FF), out_grad, gate_weights.T, routes.T, momentum)
    return pl.pallas_call(
        newton,
        out_shape=(
            jax.ShapeDtypeStruct((ROWS, FF), BF16),
            jax.ShapeDtypeStruct((ROWS, FF), F32),
        ),
        in_specs=[hbm, hbm, hbm],
        out_specs=(vmem, hbm),
        scratch_shapes=[
            pltpu.VMEM((ROWS, FF), BF16),
            pltpu.VMEM((2, 3, BLK, BLK), BF16),
            pltpu.VMEM((FF, FF), BF16),
            pltpu.VMEM((FF, FF), BF16),
            pltpu.VMEM((FF, FF), F32),
            pltpu.VMEM((FF, FF), BF16),
            pltpu.VMEM((ROWS, FF), BF16),
            pltpu.VMEM((ROWS, FF), F32),
            dma((3,)),
        ],
        compiler_params=pltpu.CompilerParams(vmem_limit_bytes=60 * 2**20),
    )(xs, gram_tot, moved)


def solution(mesh):
    in_specs = (
        P(("dp", "expert"), None, None),
        P(("dp", "expert"), None),
        P(("dp", "expert"), None),
        P(("dp", "expert"), None),
        P(("expert", "dp"), None),
    )
    out_specs = (P(("expert", "dp"), None), P(("expert", "dp"), None))
    return jax.shard_map(body, mesh=mesh, in_specs=in_specs, out_specs=out_specs, check_vma=False)
```
